32 devices in a mesh: dp: 2 (over x), ctx: 4 (over z), tp: 4 (over y, core).
Axes of the slice: x: 2, y: 2, z: 4, core: 2. Of those that a mesh axis runs over, the one named last changes fastest.
Arguments:
- routed_experts: int32 [512, 8], P(('dp', 'ctx', 'tp')), may hold values from 0 to 15, all different within a row; in each aligned block of 16 rows (0 to 15, 16 to 31, ...) at most 9 rows name the same one
- route_gates: float32 [512, 8], P(('dp', 'ctx', 'tp')), may hold values from 0.03 to 0.4
- expert_hidden: bfloat16 [16, 2, 16, 9, 768], P(('ctx', 'tp'), 'dp'), may hold values from -6 to 6
- down_weight: bfloat16 [16, 768, 4096], P(('ctx', 'tp'), None, 'dp'), may hold values from -0.21875 to 0.21875
- output_grad: bfloat16 [512, 4096], P(('dp', 'ctx', 'tp')), may hold values from -1.5 to 1.5
Outputs:
- combined: bfloat16 [512, 4096], P(('dp', 'ctx', 'tp'))
- down_gradient: float32 [16, 768, 4096], P(('ctx', 'tp'), None, 'dp')
The draws below stay inside these ranges and needn't reach their ends.
Inputs may be any that keep to these rules, and one draw needn't show every extreme that they name: `routed_experts`: each row names 8 different experts. Among the routes of one device's 16 tokens (aligned blocks of rows) no expert is named more than 9 times, and in every draw some block names some expert exactly 9 times.
All inputs are finite; a program needn't handle non-finite values.
Results may differ from the reference program's by a relative error of at most 0.0049.
Values may be sent and summed in bfloat16 or wider, within the bound.
A program may use at most 64 MiB of HBM per device.

```python
import math
import jax
import jax.numpy as jnp
import numpy as np
from jax import lax

D = 4096
FF = 768
TOPK = 8
TOK_OWN = 16
REPLICAS = 2
SOURCES = 16
EXPERTS = 16
CAP = 9
TOKENS = 512
N_DP = 2


def levels(rng, dims, shards, smallest, largest):
    factor_of, own = 1.0, jax.random.fold_in(rng, 6)
    for position, shards_of in shards:
        steps = jnp.exp(jax.random.uniform(jax.random.fold_in(own, position), (shards_of,), jnp.float32, smallest / len(shards), largest / len(shards)))
        factor_of = factor_of * jnp.repeat(steps, dims[position] // shards_of).reshape([-1 if axis == position else 1 for axis in range(len(dims))])
    return factor_of


def routed_block(own_key, own, number, rows, number_of, top, bound, slope):
    ranking = jax.random.permutation(own_key, number_of)
    crowded, usual = load_shares(number_of, rows * top, bound, slope, True), load_shares(number_of, rows * top, bound, slope, False)
    places = jnp.arange(number_of)

    def named(sizes, rotation):
        used = int((sizes > 0).sum())
        fixed = max(1, used // 4)
        shifted = fixed + (places - fixed + rotation * (used - fixed)) % max(1, number_of - fixed)
        return jnp.zeros((number_of,), jnp.int32).at[ranking[jnp.where(places < fixed, places, shifted)]].set(jnp.asarray(sizes, jnp.int32))

    sizes = jnp.where(number % 4 == 0, named(crowded, number // 4), named(usual, number - number // 4 - 1))
    mixed = jax.random.permutation(jax.random.fold_in(own, 3), number_of)
    source_of, taker = mixed[0:number_of // 2 * 2:2], mixed[1:number_of // 2 * 2:2]
    room = jnp.minimum(sizes[source_of] - 1, bound - sizes[taker]) // 2
    room = jnp.where((source_of == ranking[0]) | (taker == ranking[0]) | (sizes[taker] == 0), 0, jnp.maximum(room, 0))
    shifted = jax.random.randint(jax.random.fold_in(own, 4), (number_of // 2,), 0, 1 << 20) % (room + 1)
    sizes = sizes.at[source_of].add(-shifted).at[taker].add(shifted)
    members = jnp.searchsorted(jnp.cumsum(sizes), jnp.arange(rows * top), side="right").astype(jnp.int32)
    grid = members.reshape(top, rows).T
    grid = grid[jax.random.permutation(jax.random.fold_in(own, 1), rows)]
    rotation = jax.random.randint(jax.random.fold_in(own, 2), (rows, 1), 0, top)
    return jnp.take_along_axis(grid, (jnp.arange(top)[None, :] + rotation) % top, axis=1)


def load_shares(amount, total, bound, lean, full):
    weights = [(1 << 20) // math.isqrt(grade ** lean) + 1 for grade in range(1, amount + 1)]
    largest = bound if full else min(bound, max(-(-total // amount), total * weights[0] // sum(weights)))
    least = 1 if total - largest >= amount - 1 else 0
    counts, spare = [largest] + [least] * (amount - 1), total - largest - least * (amount - 1)
    while spare > 0:
        free = [i for i in range(1, amount) if counts[i] < largest] or [i for i in range(1, amount) if counts[i] < bound]
        mass, budget = sum([weights[i] for i in free]), spare
        for i in free:
            extra = min(bound - counts[i], max(1, budget * weights[i] // mass), spare)
            counts[i] = counts[i] + extra
            spare = spare - extra
    return np.array(counts)


def noise(own_key, dims, width, most, pieces=(), held_as=jnp.bfloat16):
    drawn = width * jax.random.normal(own_key, dims, jnp.float32)
    if pieces:
        drawn = drawn * levels(own_key, dims, pieces, -0.22, 0.18)
    return jnp.clip(drawn, -most, most).astype(held_as)


def setup_inputs(seed: int = 0) -> dict:
    splits = jax.random.split(jax.random.key(seed), 6)
    routed_experts_keys = jax.random.split(jax.random.fold_in(splits[0], 1), TOKENS // TOK_OWN)
    routed_experts_turns = jax.random.permutation(jax.random.fold_in(splits[0], 3), TOKENS // TOK_OWN)
    routed_experts = jax.vmap(lambda own, number: routed_block(jax.random.fold_in(splits[0], 2), own, number, TOK_OWN, EXPERTS, TOPK, CAP, 2))(routed_experts_keys, routed_experts_turns).reshape((TOKENS, TOPK))
    route_gates = jnp.clip(jnp.exp(math.log(0.4) - 2.5902672 * jax.random.uniform(splits[1], (TOKENS, TOPK), jnp.float32) ** levels(splits[1], (TOKENS, TOPK), ((0, 32),), -0.2, 0.2)), 0.03, 0.4)
    expert_hidden = noise(splits[2], (EXPERTS, REPLICAS, SOURCES, CAP, FF), 1.0, 6.0, ((0, 16), (1, 2)))
    down_weight = noise(splits[3], (EXPERTS, FF, D), FF ** -0.5, 0.21875, ((0, 16), (2, 2)))
    output_grad = noise(splits[4], (TOKENS, D), 0.25, 1.5, ((0, 32),))
    return dict(routed_experts=routed_experts, route_gates=route_gates, expert_hidden=expert_hidden, down_weight=down_weight, output_grad=output_grad)


def slot_table(routed_experts):
    routes = TOK_OWN * TOPK
    flat_experts = routed_experts.reshape(N_DP * SOURCES, routes)
    same = flat_experts[:, :, None] == flat_experts[:, None, :]
    order = jnp.arange(routes, dtype=jnp.int32)
    before = order[None, :] < order[:, None]
    ranks = jnp.sum(jnp.logical_and(same, before[None]), axis=2).astype(jnp.int32)
    return flat_experts, ranks


def reference(routed_experts, route_gates, expert_hidden, down_weight, output_grad):
    routes = TOK_OWN * TOPK
    rows_per = N_DP * SOURCES * CAP
    flat_experts, ranks = slot_table(routed_experts)
    device = jnp.arange(N_DP * SOURCES, dtype=jnp.int32)
    slots = device[:, None] * CAP + ranks
    whole = (flat_experts * rows_per + slots).reshape(-1)
    token = (device[:, None] * TOK_OWN + jnp.arange(routes, dtype=jnp.int32)[None, :] // TOPK).reshape(-1)
    slot_token = jnp.full((EXPERTS * rows_per,), TOKENS, jnp.int32).at[whole].set(token).reshape(EXPERTS, rows_per)
    slot_gate = jnp.zeros((EXPERTS * rows_per,), jnp.float32).at[whole].set(route_gates.reshape(-1)).reshape(EXPERTS, rows_per)
    padded_grad = jnp.concatenate([output_grad, jnp.zeros((1, D), output_grad.dtype)], axis=0)

    def one_expert(mixed, items):
        hidden_block, weight_block, token_block, gate_block = items
        rows = hidden_block.reshape(rows_per, FF)
        produced = jnp.dot(rows, weight_block, preferred_element_type=jnp.float32).astype(jnp.bfloat16)
        mixed = mixed.at[token_block].add(gate_block[:, None] * produced.astype(jnp.float32), mode="drop")
        scaled = (gate_block[:, None] * padded_grad[token_block].astype(jnp.float32)).astype(jnp.bfloat16)
        gradient = jnp.dot(rows.T, scaled, preferred_element_type=jnp.float32)
        return mixed, gradient

    mixed, gradients = lax.scan(one_expert, jnp.zeros((TOKENS, D), jnp.float32), (expert_hidden, down_weight, slot_token, slot_gate))
    return mixed.astype(jnp.bfloat16), gradients
```

```python
import functools

import jax
import jax.numpy as jnp
import numpy as np
from jax import lax
from jax.experimental import pallas as pl
from jax.experimental.pallas import tpu as pltpu
from jax.sharding import PartitionSpec as P


def slot_ranks(flat_experts):
    count = flat_experts.shape[-1]
    same = flat_experts[..., :, None] == flat_experts[..., None, :]
    before = lax.broadcasted_iota(jnp.int32, (count, count), 1) < lax.broadcasted_iota(
        jnp.int32, (count, count), 0
    )
    return jnp.sum(jnp.logical_and(same, before), axis=-1)


def expert_move(buffer):
    return lax.all_to_all(buffer, ("ctx", "tp"), split_axis=0, concat_axis=0, tiled=True)


def body(routed_experts, route_gates, expert_hidden, down_weight, output_grad):
    replicas = lax.axis_size("dp")
    sources = lax.axis_size("ctx") * lax.axis_size("tp")
    tok_own, topk = routed_experts.shape
    routes = tok_own * topk
    capacity = expert_hidden.shape[3]
    width = output_grad.shape[1]
    column_part = width // replicas
    hidden_rows = expert_hidden[0]
    weight = down_weight[0]
    slot_count = sources * capacity
    expert_table, gate_table = (
        lax.all_gather(routed_experts.astype(jnp.float32), "dp", axis=0, tiled=True),
        lax.all_gather(route_gates, "dp", axis=0, tiled=True),
    )
    all_experts = expert_table.astype(jnp.int32).reshape(replicas, routes)
    all_gates = gate_table.reshape(replicas, tok_own, topk)
    grad_columns = lax.all_to_all(
        output_grad, "dp", split_axis=1, concat_axis=0, tiled=True
    ).reshape(replicas, tok_own, 1, column_part)
    ranks = slot_ranks(all_experts)
    target = all_experts * capacity + ranks
    placer = (
        lax.broadcasted_iota(jnp.int32, (1, slot_count, routes), 1) == target[:, None, :]
    ).astype(jnp.bfloat16)
    scaled = (
        (all_gates[:, :, :, None] * grad_columns.astype(jnp.float32))
        .reshape(replicas, routes, column_part)
        .astype(jnp.bfloat16)
    )
    outgoing = jnp.einsum("rpq,rqd->prd", placer, scaled, preferred_element_type=jnp.float32)
    outgoing = outgoing.astype(jnp.bfloat16).reshape(sources, capacity, replicas, column_part)
    grad_rows = expert_move(outgoing)
    piece = lax.all_gather(hidden_rows, "dp", axis=0, tiled=True)
    produced = jnp.einsum(
        "rsjf,fd->srjd", piece, weight, preferred_element_type=jnp.float32
    ).astype(jnp.bfloat16)
    outputs = produced
    gradient = jnp.einsum("rsjf,sjrd->fd", piece, grad_rows, preferred_element_type=jnp.float32)
    outputs, gradient = (outputs, gradient)
    returned = expert_move(outputs).reshape(sources * replicas * capacity, column_part)
    replica_index = lax.broadcasted_iota(jnp.int32, (replicas, routes), 0)
    position = all_experts * (replicas * capacity) + replica_index * capacity + ranks
    picked = (
        jnp.take(returned, position, axis=0)
        .astype(jnp.float32)
        .reshape(replicas, tok_own, topk, column_part)
    )
    partial_rows = jnp.sum(all_gates[:, :, :, None] * picked, axis=2).astype(jnp.bfloat16)
    combined = lax.all_to_all(partial_rows, "dp", split_axis=0, concat_axis=2, tiled=True)[0]
    return (combined, gradient[None])


MESH = pl.DeviceIdType.MESH


def gate_parts(gates):
    high = lax.reduce_precision(gates, 8, 7)
    middle = lax.reduce_precision(gates - high, 8, 7)
    return high, middle, gates - high - middle


def fused_kernel(
    sizes, table_ref, grad_ref, hidden_ref, weight_ref, base_ref, lower_ref,
    combined_ref, tokens_ref, scaled_ref,
    cut, rows, hidden, gate_col, part, core_out, core_in, y_out, y_in, z_out, z_in, last, halves,
    dp_send, dp_recv, z_send, z_recv, y_send, y_recv, c_send, c_recv,
    rc_send, rc_recv, ry_send, ry_recv, rz_send, rz_recv, rd_send, rd_recv,
):
    tok, topk, depth, lanes, ff, width, step = sizes
    d, z, t = lax.axis_index("dp"), lax.axis_index("ctx"), lax.axis_index("tp")
    core = lax.rem(t, 2)
    y = lax.div(t, 2)
    other = {"dp": 1 - d}
    y_peer = (1 - y) * 2 + core
    c_peer = y * 2 + 1 - core
    per = depth * 2 * tok
    block = 2 * tok

    def at_z(k):
        return lax.rem(z + k, depth)

    def back(k):
        return lax.rem(z - k + depth, depth)

    def move(src, dst, send, recv, to):
        return pltpu.make_async_remote_copy(
            src_ref=src, dst_ref=dst, send_sem=send, recv_sem=recv,
            device_id=to, device_id_type=MESH)

    barrier = pltpu.get_barrier_semaphore()
    peers = [other, {"tp": y_peer}, {"tp": c_peer}] + [{"ctx": at_z(k)} for k in range(1, depth)]
    for peer in peers:
        pl.semaphore_signal(barrier, inc=1, device_id=peer, device_id_type=MESH)
    for half in range(2):
        cut[half, :, :width] = grad_ref[:, half * width:(half + 1) * width]
        cut[half, :, width:] = table_ref[...]
    rows[t, z, d] = cut[d]
    hidden[d] = hidden_ref[...]
    pl.semaphore_wait(barrier, len(peers))

    swap = move(cut.at[1 - d], rows.at[t, z, d], dp_send.at[0], dp_recv.at[0], other)
    swap.start()
    share = move(hidden_ref, hidden.at[d], dp_send.at[1], dp_recv.at[1], other)
    share.start()
    swap.wait_recv()
    z_moves, y_moves, c_moves = [], [], []
    for k in range(1, depth):
        z_moves.append(move(rows.at[t, z], rows.at[t, z], z_send.at[k], z_recv.at[k], {"ctx": at_z(k)}))
        z_moves[-1].start()
    for k in range(depth):
        own = rows.at[t, back(k)]
        if k:
            z_moves[k - 1].wait_recv()
        y_moves.append(move(own, own, y_send.at[k], y_recv.at[k], {"tp": y_peer}))
        y_moves[-1].start()
        c_moves.append(move(own, own, c_send.at[k], c_recv.at[k], {"tp": c_peer}))
        c_moves[-1].start()
    for k in range(depth):
        y_moves[k].wait_recv()
        own = rows.at[y_peer, back(k)]
        c_moves.append(move(own, own, c_send.at[depth + k], c_recv.at[depth + k], {"tp": c_peer}))
        c_moves[-1].start()
    for copy in c_moves:
        copy.wait_recv()
    share.wait_recv()

    expert = (z * lanes + t).astype(jnp.float32)
    tokens = rows.shape[0] * per
    table = rows[:, :, :, :, width:].reshape(tokens, 128).astype(jnp.float32)
    lane = lax.broadcasted_iota(jnp.int32, (tokens, 128), 1)
    named = jnp.where(jnp.logical_and(lane < topk, table == expert), 1.0, 0.0)
    spread = pltpu.roll(named, topk, 1) + pltpu.roll(named, 2 * topk, 1) + pltpu.roll(named, 3 * topk, 1)
    gate_col[...] = jnp.sum(spread * table, axis=1, keepdims=True)
    before = jnp.dot(lower_ref[...], named.astype(jnp.bfloat16), preferred_element_type=jnp.float32)
    rank = jnp.sum(before, axis=1, keepdims=True)
    slot = jnp.where(jnp.sum(named, axis=1, keepdims=True) > 0.5, base_ref[...] + rank, -1.0)
    slots = 2 * hidden.shape[1]
    place = lax.broadcasted_iota(jnp.int32, (tokens, slots), 1).astype(jnp.float32)
    placer = jnp.where(place == slot, 1.0, 0.0).astype(jnp.bfloat16)
    picked = jnp.dot(placer, hidden[...].reshape(slots, ff), preferred_element_type=jnp.float32)
    tokens_ref[...] = picked.astype(jnp.bfloat16).reshape(tokens_ref.shape)

    def forward(group, out):
        left = tokens_ref[group]
        gate = gate_col[pl.ds(pl.multiple_of(group * per, per), per), :]

        @pl.loop(0, width // step)
        def _(c):
            columns = pl.ds(pl.multiple_of(c * step, step), step)
            made = jnp.dot(left, weight_ref[:, columns], preferred_element_type=jnp.float32)
            made = made.astype(jnp.bfloat16).astype(jnp.float32) * gate
            out[:, columns] = made.astype(out.dtype)

    core_moves = []
    for i, side in enumerate((1 - y, y)):
        forward(side * 2 + 1 - core, core_out.at[i])
        core_moves.append(move(core_out.at[i], core_in.at[i], rc_send.at[i], rc_recv.at[i], {"tp": c_peer}))
        core_moves[-1].start()
    for i, side in enumerate((1 - y, y)):
        forward(side * 2 + core, part.at[i])
    back_moves = []
    core_moves[0].wait_recv()
    for k in range(depth):
        where = at_z(k + 1)
        span = pl.ds(pl.multiple_of(where * block, block), block)
        y_out[k] = (part[0, span] + core_in[0, span].astype(jnp.float32)).astype(jnp.bfloat16)
        back_moves.append(move(y_out.at[k], y_in.at[k], ry_send.at[k], ry_recv.at[k], {"tp": y_peer}))
        back_moves[-1].start()

    core_moves[1].wait_recv()

    @pl.loop(0, tokens // block)
    def _(c):
        span = pl.ds(pl.multiple_of(c * block, block), block)
        gate = gate_col[span, :]
        grads = rows[lax.div(c, depth), lax.rem(c, depth)][:, :, :width].reshape(block, width)
        scaled_ref[span, :] = (gate * grads.astype(jnp.float32)).astype(jnp.bfloat16)

    out_moves = []
    for k in range(depth):
        where = at_z(k + 1)
        span = pl.ds(pl.multiple_of(where * block, block), block)
        back_moves[k].wait_recv()
        total = part[1, span] + core_in[1, span].astype(jnp.float32) + y_in[k].astype(jnp.float32)
        if k < depth - 1:
            z_out[k] = total.astype(jnp.bfloat16)
            out_moves.append(move(z_out.at[k], z_in.at[k], rz_send.at[k], rz_recv.at[k], {"ctx": where}))
            out_moves[-1].start()
    for k in range(depth - 1):
        out_moves[k].wait_recv()
        total = total + z_in[k].astype(jnp.float32)
    for r in range(2):
        last[r] = total[r * tok:(r + 1) * tok].astype(jnp.bfloat16)
    halves[d] = last[d]
    finish = move(last.at[1 - d], halves.at[d], rd_send, rd_recv, other)
    finish.start()
    finish.wait_recv()
    for half in range(2):
        combined_ref[:, half * width:(half + 1) * width] = halves[half]
    for copy in [swap, share, finish] + z_moves + y_moves + c_moves + core_moves + back_moves + out_moves:
        copy.wait_send()


def fused_body(routed_experts, route_gates, expert_hidden, down_weight, output_grad):
    depth, lanes = lax.axis_size("ctx"), lax.axis_size("tp")
    tok, topk = routed_experts.shape
    capacity, ff = expert_hidden.shape[3:]
    slots = depth * lanes * capacity
    width = output_grad.shape[1] // 2
    tokens = 2 * depth * lanes * tok
    per = tokens // lanes
    step = 512 if width % 512 == 0 else width
    table = jnp.concatenate([routed_experts.astype(jnp.float32), *gate_parts(route_gates)], axis=1)
    table = jnp.pad(table, ((0, 0), (0, 128 - 4 * topk))).astype(jnp.bfloat16)
    index = np.arange(tokens)
    place = index // tok
    source = place % 2 * (depth * lanes) + place // 2 % depth * lanes + place // (2 * depth)
    base = jnp.asarray((source * capacity)[:, None], jnp.float32)
    lower = jnp.asarray((place[:, None] == place[None]) & (index[None] < index[:, None]), jnp.bfloat16)
    vmem = pl.BlockSpec(memory_space=pltpu.VMEM)
    wide, half = width + 128, jnp.bfloat16
    dma = pltpu.SemaphoreType.DMA
    combined, picked, scaled = pl.pallas_call(
        functools.partial(fused_kernel, (tok, topk, depth, lanes, ff, width, step)),
        out_shape=(
            jax.ShapeDtypeStruct(output_grad.shape, half),
            jax.ShapeDtypeStruct((lanes, per, ff), half),
            jax.ShapeDtypeStruct((tokens, width), half),
        ),
        in_specs=[vmem] * 6,
        out_specs=[vmem] * 3,
        scratch_shapes=[
            pltpu.VMEM((2, tok, wide), half),
            pltpu.VMEM((lanes, depth, 2, tok, wide), half),
            pltpu.VMEM((2, slots, ff), half),
            pltpu.VMEM((tokens, 1), jnp.float32),
            pltpu.VMEM((2, per, width), jnp.float32),
            pltpu.VMEM((2, per, width), half),
            pltpu.VMEM((2, per, width), half),
            pltpu.VMEM((depth, 2 * tok, width), half),
            pltpu.VMEM((depth, 2 * tok, width), half),
            pltpu.VMEM((depth, 2 * tok, width), half),
            pltpu.VMEM((depth, 2 * tok, width), half),
            pltpu.VMEM((2, tok, width), half),
            pltpu.VMEM((2, tok, width), half),
            dma((2,)), dma((2,)), dma((depth,)), dma((depth,)), dma((depth,)), dma((depth,)),
            dma((2 * depth,)), dma((2 * depth,)),
            dma((2,)), dma((2,)), dma((depth,)), dma((depth,)), dma((depth,)), dma((depth,)), dma, dma,
        ],
        compiler_params=pltpu.CompilerParams(
            collective_id=0, has_side_effects=True, vmem_limit_bytes=40 * 1024 * 1024),
    )(table, output_grad, expert_hidden.reshape(slots, ff), down_weight[0], base, lower)
    gradient = lax.dot_general(
        picked.reshape(tokens, ff), scaled, (((0,), (0,)), ((), ())), preferred_element_type=jnp.float32)
    return combined, gradient[None]


def solution(mesh):
    in_specs = (
        P(("dp", "ctx", "tp"), None),
        P(("dp", "ctx", "tp"), None),
        P(("ctx", "tp"), "dp", None, None, None),
        P(("ctx", "tp"), None, "dp"),
        P(("dp", "ctx", "tp"), None),
    )
    out_specs = (P(("dp", "ctx", "tp"), None), P(("ctx", "tp"), None, "dp"))
    pairs = mesh.shape["dp"] == 2 and mesh.shape["tp"] == 4
    return jax.shard_map(fused_body if pairs else body, mesh=mesh, in_specs=in_specs, out_specs=out_specs, check_vma=False)
```

```python
import functools

import jax
import jax.numpy as jnp
from jax import lax
from jax.experimental import pallas as pl
from jax.experimental.pallas import tpu as pltpu
from jax.sharding import PartitionSpec as P


def slot_ranks(flat_experts):
    count = flat_experts.shape[-1]
    same = flat_experts[..., :, None] == flat_experts[..., None, :]
    before = lax.broadcasted_iota(jnp.int32, (count, count), 1) < lax.broadcasted_iota(
        jnp.int32, (count, count), 0
    )
    return jnp.sum(jnp.logical_and(same, before), axis=-1)


def expert_move(buffer):
    return lax.all_to_all(buffer, ("ctx", "tp"), split_axis=0, concat_axis=0, tiled=True)


def body(routed_experts, route_gates, expert_hidden, down_weight, output_grad):
    replicas = lax.axis_size("dp")
    sources = lax.axis_size("ctx") * lax.axis_size("tp")
    tok_own, topk = routed_experts.shape
    routes = tok_own * topk
    capacity = expert_hidden.shape[3]
    width = output_grad.shape[1]
    column_part = width // replicas
    hidden_rows = expert_hidden[0]
    weight = down_weight[0]
    slot_count = sources * capacity
    expert_table, gate_table = (
        lax.all_gather(routed_experts.astype(jnp.float32), "dp", axis=0, tiled=True),
        lax.all_gather(route_gates, "dp", axis=0, tiled=True),
    )
    all_experts = expert_table.astype(jnp.int32).reshape(replicas, routes)
    all_gates = gate_table.reshape(replicas, tok_own, topk)
    grad_columns = lax.all_to_all(
        output_grad, "dp", split_axis=1, concat_axis=0, tiled=True
    ).reshape(replicas, tok_own, 1, column_part)
    ranks = slot_ranks(all_experts)
    target = all_experts * capacity + ranks
    placer = (
        lax.broadcasted_iota(jnp.int32, (1, slot_count, routes), 1) == target[:, None, :]
    ).astype(jnp.bfloat16)
    scaled = (
        (all_gates[:, :, :, None] * grad_columns.astype(jnp.float32))
        .reshape(replicas, routes, column_part)
        .astype(jnp.bfloat16)
    )
    outgoing = jnp.einsum("rpq,rqd->prd", placer, scaled, preferred_element_type=jnp.float32)
    outgoing = outgoing.astype(jnp.bfloat16).reshape(sources, capacity, replicas, column_part)
    grad_rows = expert_move(outgoing)
    piece = lax.all_gather(hidden_rows, "dp", axis=0, tiled=True)
    produced = jnp.einsum(
        "rsjf,fd->srjd", piece, weight, preferred_element_type=jnp.float32
    ).astype(jnp.bfloat16)
    outputs = produced
    gradient = jnp.einsum("rsjf,sjrd->fd", piece, grad_rows, preferred_element_type=jnp.float32)
    outputs, gradient = (outputs, gradient)
    returned = expert_move(outputs).reshape(sources * replicas * capacity, column_part)
    replica_index = lax.broadcasted_iota(jnp.int32, (replicas, routes), 0)
    position = all_experts * (replicas * capacity) + replica_index * capacity + ranks
    picked = (
        jnp.take(returned, position, axis=0)
        .astype(jnp.float32)
        .reshape(replicas, tok_own, topk, column_part)
    )
    partial_rows = jnp.sum(all_gates[:, :, :, None] * picked, axis=2).astype(jnp.bfloat16)
    combined = lax.all_to_all(partial_rows, "dp", split_axis=0, concat_axis=2, tiled=True)[0]
    return (combined, gradient[None])


MESH = pl.DeviceIdType.MESH


def fused_kernel(
    sizes, routes_ref, gates_ref, grad_ref, hidden_ref, weight_ref,
    combined_ref, tokens_ref, scaled_ref,
    stack, tables, rows, hidden, weight, base, lower, gate_col,
    part, core_out, core_in, y_out, y_in, z_out, z_in, last, halves,
    local_sem, dp_send, dp_recv, tz_send, tz_recv, ty_send, ty_recv, tc_send, tc_recv,
    z_send, z_recv, y_send, y_recv, c_send, c_recv,
    rc_send, rc_recv, ry_send, ry_recv, rz_send, rz_recv,
):
    tok, topk, depth, lanes, ff, width, step = sizes
    d, z, t = lax.axis_index("dp"), lax.axis_index("ctx"), lax.axis_index("tp")
    core = lax.rem(t, 2)
    y = lax.div(t, 2)
    other = {"dp": 1 - d}
    y_peer = {"tp": (1 - y) * 2 + core}
    c_peer = {"tp": y * 2 + 1 - core}
    here, across = core * 2 + y, core * 2 + 1 - y
    per = depth * 2 * tok
    block = 2 * tok
    tokens = lanes * per

    def at_z(k):
        return lax.rem(z + k, depth)

    def back(k):
        return lax.rem(z - k + depth, depth)

    def send(src, dst, send_sem, recv_sem, to):
        copy = pltpu.make_async_remote_copy(
            src_ref=src, dst_ref=dst, send_sem=send_sem, recv_sem=recv_sem,
            device_id=to, device_id_type=MESH)
        copy.start()
        return copy

    def columns_of(half):
        return grad_ref.at[:, pl.ds(pl.multiple_of(half * width, 128), width)]

    barrier = pltpu.get_barrier_semaphore()
    peers = [other, y_peer, c_peer] + [{"ctx": at_z(k)} for k in range(1, depth)]
    for peer in peers:
        pl.semaphore_signal(barrier, inc=1, device_id=peer, device_id_type=MESH)
    local = []
    for i, (src, dst) in enumerate((
        (columns_of(d), rows.at[here, z, d]), (hidden_ref, hidden.at[d]),
        (weight_ref, weight),
    )):
        local.append(pltpu.make_async_copy(src, dst, local_sem.at[i]))
        local[-1].start()
    gates = gates_ref[...]
    high = gates.astype(jnp.bfloat16).astype(jnp.float32)
    middle = (gates - high).astype(jnp.bfloat16).astype(jnp.float32)
    stack[0:topk] = routes_ref[...].astype(jnp.float32)
    stack[topk:2 * topk] = high
    stack[2 * topk:3 * topk] = middle
    stack[3 * topk:] = gates - high - middle
    spread_rows = lax.broadcasted_iota(jnp.int32, (4 * topk, 128), 0)
    spread_lanes = lax.broadcasted_iota(jnp.int32, (4 * topk, 128), 1)
    spreader = jnp.where(spread_rows == spread_lanes, 1.0, 0.0).astype(jnp.bfloat16)
    tables[here, z, d] = lax.dot_general(
        stack[...].astype(jnp.bfloat16), spreader, (((0,), (0,)), ((), ())),
        preferred_element_type=jnp.float32).astype(jnp.bfloat16)
    pl.semaphore_wait(barrier, len(peers))

    own = tables.at[here, z, d]
    sent = [send(own, own, dp_send.at[0], dp_recv.at[0], other)]
    sent.append(send(columns_of(1 - d), rows.at[here, z, d], dp_send.at[1], dp_recv.at[1], other))
    sent.append(send(hidden_ref, hidden.at[d], dp_send.at[2], dp_recv.at[2], other))

    def spread_z(buffer, sends, recvs):
        own = buffer.at[here, z]
        return [send(own, own, sends.at[k], recvs.at[k], {"ctx": at_z(k)}) for k in range(1, depth)]

    def hand(buffer, group, k, slot, sends, recvs, to):
        own = buffer.at[group, back(k)]
        return send(own, own, sends.at[slot], recvs.at[slot], to)

    sources = depth * lanes
    for q in range(lanes):
        for k in range(2 * depth):
            origin = k % 2 * (sources * (hidden.shape[1] // sources)) + k // 2 * lanes + q % 2 * 2 + q // 2
            start = q * per + k * tok
            base[start:start + tok] = jnp.full((tok, 1), float(origin), jnp.float32)
    lower_rows = lax.broadcasted_iota(jnp.int32, (tok, tokens), 0)
    lower_lanes = lax.broadcasted_iota(jnp.int32, (tok, tokens), 1)

    @pl.loop(0, tokens // tok)
    def _(c):
        earlier = jnp.logical_and(lower_lanes >= c * tok, lower_lanes < lower_rows + c * tok)
        lower[pl.ds(pl.multiple_of(c * tok, tok), tok), :] = jnp.where(earlier, 1.0, 0.0).astype(jnp.bfloat16)

    sent[0].wait_recv()
    tz = spread_z(tables, tz_send, tz_recv)
    ty, tc, yy, cc = [], [], [], []
    ty.append(hand(tables, here, 0, 0, ty_send, ty_recv, y_peer))
    tc.append(hand(tables, here, 0, 0, tc_send, tc_recv, c_peer))
    local[0].wait()
    sent[1].wait_recv()
    zz = spread_z(rows, z_send, z_recv)
    yy.append(hand(rows, here, 0, 0, y_send, y_recv, y_peer))
    cc.append(hand(rows, here, 0, 0, c_send, c_recv, c_peer))
    for k in range(1, depth):
        tz[k - 1].wait_recv()
        ty.append(hand(tables, here, k, k, ty_send, ty_recv, y_peer))
        tc.append(hand(tables, here, k, k, tc_send, tc_recv, c_peer))
    for k in range(depth):
        ty[k].wait_recv()
        tc.append(hand(tables, across, k, depth + k, tc_send, tc_recv, c_peer))
    for copy in tc:
        copy.wait_recv()

    expert = (z * lanes + t).astype(jnp.float32)
    table = tables[...].reshape(tokens, 128).astype(jnp.float32)
    lane = lax.broadcasted_iota(jnp.int32, (tokens, 128), 1)
    named = jnp.where(jnp.logical_and(lane < topk, table == expert), 1.0, 0.0)
    spread = pltpu.roll(named, topk, 1) + pltpu.roll(named, 2 * topk, 1) + pltpu.roll(named, 3 * topk, 1)
    gate_col[...] = jnp.sum(spread * table, axis=1, keepdims=True)
    before = jnp.dot(lower[...], named.astype(jnp.bfloat16), preferred_element_type=jnp.float32)
    rank = jnp.sum(before, axis=1, keepdims=True)
    used = jnp.sum(named, axis=1, keepdims=True) > 0.5
    slot = jnp.where(used, base[...] + rank * (depth * lanes), -1.0)
    slots = 2 * hidden.shape[1]
    place = lax.broadcasted_iota(jnp.int32, (tokens, slots), 1).astype(jnp.float32)
    placer = jnp.where(place == slot, 1.0, 0.0).astype(jnp.bfloat16)
    local[1].wait()
    sent[2].wait_recv()
    picked = jnp.dot(placer, hidden[...].reshape(slots, ff), preferred_element_type=jnp.float32)
    tokens_ref[...] = picked.astype(jnp.bfloat16).reshape(tokens_ref.shape)
    local[2].wait()

    def forward(side, out):
        left = tokens_ref[side]
        gate = gate_col[pl.ds(pl.multiple_of(side * 2 * per, per), 2 * per), :]

        @pl.loop(0, width // step)
        def _(c):
            columns = pl.ds(pl.multiple_of(c * step, step), step)
            made = jnp.dot(left, weight[:, columns], preferred_element_type=jnp.float32)
            made = made.astype(jnp.bfloat16).astype(jnp.float32) * gate
            for half in range(2):
                out[half, :, columns] = made[half * per:(half + 1) * per].astype(out.dtype)

    forward(1 - core, core_out)
    core_moves = []
    for i, side in enumerate((1 - y, y)):
        core_moves.append(send(core_out.at[side], core_in.at[side], rc_send.at[i], rc_recv.at[i], c_peer))
    for k in range(1, depth):
        zz[k - 1].wait_recv()
        yy.append(hand(rows, here, k, k, y_send, y_recv, y_peer))
        cc.append(hand(rows, here, k, k, c_send, c_recv, c_peer))
    forward(core, part)
    core_moves[0].wait_recv()
    back_moves = []
    for k in range(depth):
        span = pl.ds(pl.multiple_of(at_z(k + 1) * block, block), block)
        y_out[k] = (part[1 - y, span] + core_in[1 - y, span].astype(jnp.float32)).astype(jnp.bfloat16)
        back_moves.append(send(y_out.at[k], y_in.at[k], ry_send.at[k], ry_recv.at[k], y_peer))
    for k in range(depth):
        yy[k].wait_recv()
        cc.append(hand(rows, across, k, depth + k, c_send, c_recv, c_peer))
    core_moves[1].wait_recv()
    out_moves = []
    for k in range(depth):
        where = at_z(k + 1)
        span = pl.ds(pl.multiple_of(where * block, block), block)
        back_moves[k].wait_recv()
        total = part[y, span] + core_in[y, span].astype(jnp.float32) + y_in[k].astype(jnp.float32)
        if k < depth - 1:
            z_out[k] = total.astype(jnp.bfloat16)
            out_moves.append(send(z_out.at[k], z_in.at[k], rz_send.at[k], rz_recv.at[k], {"ctx": where}))
    for copy in cc:
        copy.wait_recv()

    @pl.loop(0, tokens // block)
    def _(c):
        span = pl.ds(pl.multiple_of(c * block, block), block)
        gate = gate_col[span, :]
        grads = rows[lax.div(c, depth), lax.rem(c, depth)].reshape(block, width)
        scaled_ref[span, :] = (gate * grads.astype(jnp.float32)).astype(jnp.bfloat16)

    for k in range(depth - 1):
        out_moves[k].wait_recv()
        total = total + z_in[k].astype(jnp.float32)
    for r in range(2):
        last[r] = total[r * tok:(r + 1) * tok].astype(jnp.bfloat16)
    finish = send(last.at[1 - d], halves.at[d], dp_send.at[3], dp_recv.at[3], other)
    halves[d] = last[d]
    finish.wait_recv()
    for half in range(2):
        combined_ref[:, half * width:(half + 1) * width] = halves[half]
    for copy in sent + [finish] + tz + ty + tc + zz + yy + cc + core_moves + back_moves + out_moves:
        copy.wait_send()


def fused_body(routed_experts, route_gates, expert_hidden, down_weight, output_grad):
    depth, lanes = lax.axis_size("ctx"), lax.axis_size("tp")
    tok, topk = routed_experts.shape
    capacity, ff = expert_hidden.shape[3:]
    sources = depth * lanes
    slots = sources * capacity
    width = output_grad.shape[1] // 2
    tokens = 2 * depth * lanes * tok
    per = tokens // lanes
    step = 512 if width % 512 == 0 else width
    vmem = pl.BlockSpec(memory_space=pltpu.VMEM)
    hbm = pl.BlockSpec(memory_space=pltpu.HBM)
    half = jnp.bfloat16
    dma = pltpu.SemaphoreType.DMA
    four, eight = dma((depth,)), dma((2 * depth,))
    combined, picked, scaled = pl.pallas_call(
        functools.partial(fused_kernel, (tok, topk, depth, lanes, ff, width, step)),
        out_shape=(
            jax.ShapeDtypeStruct(output_grad.shape, half),
            jax.ShapeDtypeStruct((2, 2 * per, ff), half),
            jax.ShapeDtypeStruct((tokens, width), half),
        ),
        in_specs=[vmem] * 2 + [hbm] * 3,
        out_specs=[vmem] * 3,
        scratch_shapes=[
            pltpu.VMEM((4 * topk, tok), jnp.float32),
            pltpu.VMEM((lanes, depth, 2, tok, 128), half),
            pltpu.VMEM((lanes, depth, 2, tok, width), half),
            pltpu.VMEM((2, slots, ff), half),
            pltpu.VMEM(down_weight.shape[1:], half),
            pltpu.VMEM((tokens, 1), jnp.float32),
            pltpu.VMEM((tokens, tokens), half),
            pltpu.VMEM((tokens, 1), jnp.float32),
            pltpu.VMEM((2, per, width), jnp.float32),
            pltpu.VMEM((2, per, width), half),
            pltpu.VMEM((2, per, width), half),
            pltpu.VMEM((depth, 2 * tok, width), half),
            pltpu.VMEM((depth, 2 * tok, width), half),
            pltpu.VMEM((depth, 2 * tok, width), half),
            pltpu.VMEM((depth, 2 * tok, width), half),
            pltpu.VMEM((2, tok, width), half),
            pltpu.VMEM((2, tok, width), half),
            dma((3,)), dma((4,)), dma((4,)), four, four, four, four, eight, eight,
            four, four, four, four, eight, eight,
            dma((2,)), dma((2,)), four, four, four, four,
        ],
        compiler_params=pltpu.CompilerParams(
            collective_id=0, has_side_effects=True, vmem_limit_bytes=58 * 1024 * 1024),
    )(
        routed_experts.T, route_gates.T, output_grad,
        expert_hidden[0, 0].transpose(1, 0, 2).reshape(slots, ff), down_weight[0])
    gradient = lax.dot_general(
        picked.reshape(tokens, ff), scaled, (((0,), (0,)), ((), ())), preferred_element_type=jnp.float32)
    return combined, gradient[None]


def solution(mesh):
    in_specs = (
        P(("dp", "ctx", "tp"), None),
        P(("dp", "ctx", "tp"), None),
        P(("ctx", "tp"), "dp", None, None, None),
        P(("ctx", "tp"), None, "dp"),
        P(("dp", "ctx", "tp"), None),
    )
    out_specs = (P(("dp", "ctx", "tp"), None), P(("ctx", "tp"), None, "dp"))
    pairs = mesh.shape["dp"] == 2 and mesh.shape["tp"] == 4
    return jax.shard_map(fused_body if pairs else body, mesh=mesh, in_specs=in_specs, out_specs=out_specs, check_vma=False)
```

```python
import functools

import jax
import jax.numpy as jnp
from jax import lax
from jax.experimental import pallas as pl
from jax.experimental.pallas import tpu as pltpu
from jax.sharding import PartitionSpec as P


def slot_ranks(flat_experts):
    count = flat_experts.shape[-1]
    same = flat_experts[..., :, None] == flat_experts[..., None, :]
    before = lax.broadcasted_iota(jnp.int32, (count, count), 1) < lax.broadcasted_iota(
        jnp.int32, (count, count), 0
    )
    return jnp.sum(jnp.logical_and(same, before), axis=-1)


def expert_move(buffer):
    return lax.all_to_all(buffer, ("ctx", "tp"), split_axis=0, concat_axis=0, tiled=True)


def body(routed_experts, route_gates, expert_hidden, down_weight, output_grad):
    replicas = lax.axis_size("dp")
    sources = lax.axis_size("ctx") * lax.axis_size("tp")
    tok_own, topk = routed_experts.shape
    routes = tok_own * topk
    capacity = expert_hidden.shape[3]
    width = output_grad.shape[1]
    column_part = width // replicas
    hidden_rows = expert_hidden[0]
    weight = down_weight[0]
    slot_count = sources * capacity
    expert_table, gate_table = (
        lax.all_gather(routed_experts.astype(jnp.float32), "dp", axis=0, tiled=True),
        lax.all_gather(route_gates, "dp", axis=0, tiled=True),
    )
    all_experts = expert_table.astype(jnp.int32).reshape(replicas, routes)
    all_gates = gate_table.reshape(replicas, tok_own, topk)
    grad_columns = lax.all_to_all(
        output_grad, "dp", split_axis=1, concat_axis=0, tiled=True
    ).reshape(replicas, tok_own, 1, column_part)
    ranks = slot_ranks(all_experts)
    target = all_experts * capacity + ranks
    placer = (
        lax.broadcasted_iota(jnp.int32, (1, slot_count, routes), 1) == target[:, None, :]
    ).astype(jnp.bfloat16)
    scaled = (
        (all_gates[:, :, :, None] * grad_columns.astype(jnp.float32))
        .reshape(replicas, routes, column_part)
        .astype(jnp.bfloat16)
    )
    outgoing = jnp.einsum("rpq,rqd->prd", placer, scaled, preferred_element_type=jnp.float32)
    outgoing = outgoing.astype(jnp.bfloat16).reshape(sources, capacity, replicas, column_part)
    grad_rows = expert_move(outgoing)
    piece = lax.all_gather(hidden_rows, "dp", axis=0, tiled=True)
    produced = jnp.einsum(
        "rsjf,fd->srjd", piece, weight, preferred_element_type=jnp.float32
    ).astype(jnp.bfloat16)
    outputs = produced
    gradient = jnp.einsum("rsjf,sjrd->fd", piece, grad_rows, preferred_element_type=jnp.float32)
    outputs, gradient = (outputs, gradient)
    returned = expert_move(outputs).reshape(sources * replicas * capacity, column_part)
    replica_index = lax.broadcasted_iota(jnp.int32, (replicas, routes), 0)
    position = all_experts * (replicas * capacity) + replica_index * capacity + ranks
    picked = (
        jnp.take(returned, position, axis=0)
        .astype(jnp.float32)
        .reshape(replicas, tok_own, topk, column_part)
    )
    partial_rows = jnp.sum(all_gates[:, :, :, None] * picked, axis=2).astype(jnp.bfloat16)
    combined = lax.all_to_all(partial_rows, "dp", split_axis=0, concat_axis=2, tiled=True)[0]
    return (combined, gradient[None])


MESH = pl.DeviceIdType.MESH


def fused_kernel(
    sizes, routes_ref, gates_ref, grad_ref, hidden_ref, weight_ref,
    combined_ref, tokens_ref, scaled_ref,
    stack, tables, rows, hidden, weight, base, lower, gate_col,
    part, core_out, core_in, y_out, y_in, z_out, z_in, last, halves,
    local_sem, dp_send, dp_recv, tz_send, tz_recv, ty_send, ty_recv, tc_send, tc_recv,
    z_send, z_recv, y_send, y_recv, c_send, c_recv,
    rc_send, rc_recv, ry_send, ry_recv, rz_send, rz_recv,
):
    tok, topk, depth, lanes, ff, width, step = sizes
    d, z, t = lax.axis_index("dp"), lax.axis_index("ctx"), lax.axis_index("tp")
    core = lax.rem(t, 2)
    y = lax.div(t, 2)
    other = {"dp": 1 - d}
    y_peer = {"tp": (1 - y) * 2 + core}
    c_peer = {"tp": y * 2 + 1 - core}
    here, across = core * 2 + y, core * 2 + 1 - y
    per = depth * 2 * tok
    block = 2 * tok
    tokens = lanes * per

    def at_z(k):
        return lax.rem(z + k, depth)

    def back(k):
        return lax.rem(z - k + depth, depth)

    def send(src, dst, send_sem, recv_sem, to):
        copy = pltpu.make_async_remote_copy(
            src_ref=src, dst_ref=dst, send_sem=send_sem, recv_sem=recv_sem,
            device_id=to, device_id_type=MESH)
        copy.start()
        return copy

    def columns_of(half):
        return grad_ref.at[:, pl.ds(pl.multiple_of(half * width, 128), width)]

    barrier = pltpu.get_barrier_semaphore()
    peers = [other, y_peer, c_peer] + [{"ctx": at_z(k)} for k in range(1, depth)]
    for peer in peers:
        pl.semaphore_signal(barrier, inc=1, device_id=peer, device_id_type=MESH)
    local = []
    for i, (src, dst) in enumerate((
        (columns_of(d), rows.at[here, z, d]), (hidden_ref, hidden.at[d]),
        (weight_ref, weight),
    )):
        local.append(pltpu.make_async_copy(src, dst, local_sem.at[i]))
        local[-1].start()
    gates = gates_ref[...]
    high = gates.astype(jnp.bfloat16).astype(jnp.float32)
    middle = (gates - high).astype(jnp.bfloat16).astype(jnp.float32)
    stack[0:topk] = routes_ref[...].astype(jnp.float32)
    stack[topk:2 * topk] = high
    stack[2 * topk:3 * topk] = middle
    stack[3 * topk:] = gates - high - middle
    spread_rows = lax.broadcasted_iota(jnp.int32, (4 * topk, 128), 0)
    spread_lanes = lax.broadcasted_iota(jnp.int32, (4 * topk, 128), 1)
    spreader = jnp.where(spread_rows == spread_lanes, 1.0, 0.0).astype(jnp.bfloat16)
    tables[here, z, d] = lax.dot_general(
        stack[...].astype(jnp.bfloat16), spreader, (((0,), (0,)), ((), ())),
        preferred_element_type=jnp.float32).astype(jnp.bfloat16)
    pl.semaphore_wait(barrier, len(peers))

    own = tables.at[here, z, d]
    sent = [send(own, own, dp_send.at[0], dp_recv.at[0], other)]
    sent.append(send(columns_of(1 - d), rows.at[here, z, d], dp_send.at[1], dp_recv.at[1], other))
    sent.append(send(hidden_ref, hidden.at[d], dp_send.at[2], dp_recv.at[2], other))

    def spread_z(buffer, sends, recvs):
        own = buffer.at[here, z]
        return [send(own, own, sends.at[k], recvs.at[k], {"ctx": at_z(k)}) for k in range(1, depth)]

    def hand(buffer, group, k, slot, sends, recvs, to):
        own = buffer.at[group, back(k)]
        return send(own, own, sends.at[slot], recvs.at[slot], to)

    sources = depth * lanes
    for q in range(lanes):
        for k in range(2 * depth):
            origin = k % 2 * (sources * (hidden.shape[1] // sources)) + k // 2 * lanes + q % 2 * 2 + q // 2
            start = q * per + k * tok
            base[start:start + tok] = jnp.full((tok, 1), float(origin), jnp.float32)
    lower_rows = lax.broadcasted_iota(jnp.int32, (tok, tokens), 0)
    lower_lanes = lax.broadcasted_iota(jnp.int32, (tok, tokens), 1)

    @pl.loop(0, tokens // tok)
    def _(c):
        earlier = jnp.logical_and(lower_lanes >= c * tok, lower_lanes < lower_rows + c * tok)
        lower[pl.ds(pl.multiple_of(c * tok, tok), tok), :] = jnp.where(earlier, 1.0, 0.0).astype(jnp.bfloat16)

    def line(where, k, leftward, to):
        own = rows.at[here, where]
        slot = depth + k if leftward else k
        return pltpu.make_async_remote_copy(
            src_ref=own, dst_ref=own, send_sem=z_send.at[slot], recv_sem=z_recv.at[slot],
            device_id={"ctx": to}, device_id_type=MESH)

    def hands(group, where, slot, far):
        own = rows.at[group, where]
        mine = 2 * depth + slot if far else slot
        to_core = pltpu.make_async_remote_copy(
            src_ref=own, dst_ref=own, send_sem=c_send.at[mine], recv_sem=c_recv.at[mine],
            device_id=c_peer, device_id_type=MESH)
        if far:
            return [to_core]
        return [pltpu.make_async_remote_copy(
            src_ref=own, dst_ref=own, send_sem=y_send.at[slot], recv_sem=y_recv.at[slot],
            device_id=y_peer, device_id_type=MESH), to_core]

    def onward(where, k, slot):
        moves = []
        if slot < depth:
            moves.append((z < depth - 1, line(where, k + 1, False, at_z(1))))
        if slot >= depth or k == 0:
            moves.append((z > 0, line(where, k + 1, True, back(1))))
        return moves if k + 1 < depth else []

    def pass_on(where, k, *slots):
        for ready, copy in onward(where, k, 0) if k == 0 else onward(where, k, slots[0]):
            pl.when(ready)(copy.start)
        for copy in hands(here, where, 0 if k == 0 else slots[0], False):
            copy.start()

    def arrivals(k):
        return ((z >= k, back(k), k), (z + k < depth, at_z(k), depth + k))

    def relay(k):
        for valid, where, slot in arrivals(k):
            @pl.when(valid)
            def _(where=where, slot=slot):
                line(where, k, slot >= depth, at_z(1)).wait_recv()
                pass_on(where, k, slot)

    def each_block(act):
        act(z, 0, 0)
        for k in range(1, depth):
            for valid, where, slot in arrivals(k):
                @pl.when(valid)
                def _(where=where, slot=slot, k=k):
                    act(where, k, slot)

    sent[0].wait_recv()
    tz = spread_z(tables, tz_send, tz_recv)
    ty, tc = [], []
    ty.append(hand(tables, here, 0, 0, ty_send, ty_recv, y_peer))
    tc.append(hand(tables, here, 0, 0, tc_send, tc_recv, c_peer))
    local[0].wait()
    sent[1].wait_recv()
    pass_on(z, 0)
    for k in range(1, depth):
        tz[k - 1].wait_recv()
        ty.append(hand(tables, here, k, k, ty_send, ty_recv, y_peer))
        tc.append(hand(tables, here, k, k, tc_send, tc_recv, c_peer))
    for k in range(depth):
        ty[k].wait_recv()
        tc.append(hand(tables, across, k, depth + k, tc_send, tc_recv, c_peer))
    relay(1)
    for copy in tc:
        copy.wait_recv()

    expert = (z * lanes + t).astype(jnp.float32)
    table = tables[...].reshape(tokens, 128).astype(jnp.float32)
    lane = lax.broadcasted_iota(jnp.int32, (tokens, 128), 1)
    named = jnp.where(jnp.logical_and(lane < topk, table == expert), 1.0, 0.0)
    spread = pltpu.roll(named, topk, 1) + pltpu.roll(named, 2 * topk, 1) + pltpu.roll(named, 3 * topk, 1)
    gate_col[...] = jnp.sum(spread * table, axis=1, keepdims=True)
    before = jnp.dot(lower[...], named.astype(jnp.bfloat16), preferred_element_type=jnp.float32)
    rank = jnp.sum(before, axis=1, keepdims=True)
    used = jnp.sum(named, axis=1, keepdims=True) > 0.5
    slot = jnp.where(used, base[...] + rank * (depth * lanes), -1.0)
    slots = 2 * hidden.shape[1]
    place = lax.broadcasted_iota(jnp.int32, (tokens, slots), 1).astype(jnp.float32)
    placer = jnp.where(place == slot, 1.0, 0.0).astype(jnp.bfloat16)
    local[1].wait()
    sent[2].wait_recv()
    picked = jnp.dot(placer, hidden[...].reshape(slots, ff), preferred_element_type=jnp.float32)
    tokens_ref[...] = picked.astype(jnp.bfloat16).reshape(tokens_ref.shape)
    relay(2)
    local[2].wait()

    def forward(side, out):
        left = tokens_ref[side]
        gate = gate_col[pl.ds(pl.multiple_of(side * 2 * per, per), 2 * per), :]

        @pl.loop(0, width // step)
        def _(c):
            columns = pl.ds(pl.multiple_of(c * step, step), step)
            made = jnp.dot(left, weight[:, columns], preferred_element_type=jnp.float32)
            made = made.astype(jnp.bfloat16).astype(jnp.float32) * gate
            for half in range(2):
                out[half, :, columns] = made[half * per:(half + 1) * per].astype(out.dtype)

    forward(1 - core, core_out)
    core_moves = []
    for i, side in enumerate((1 - y, y)):
        core_moves.append(send(core_out.at[side], core_in.at[side], rc_send.at[i], rc_recv.at[i], c_peer))
    for k in range(3, depth):
        relay(k)
    forward(core, part)
    core_moves[0].wait_recv()
    back_moves = []
    for k in range(depth):
        span = pl.ds(pl.multiple_of(at_z(k + 1) * block, block), block)
        y_out[k] = (part[1 - y, span] + core_in[1 - y, span].astype(jnp.float32)).astype(jnp.bfloat16)
        back_moves.append(send(y_out.at[k], y_in.at[k], ry_send.at[k], ry_recv.at[k], y_peer))
    def cross(where, k, slot):
        hands(here, where, slot, False)[0].wait_recv()
        hands(across, where, slot, True)[0].start()

    each_block(cross)
    core_moves[1].wait_recv()
    out_moves = []
    for k in range(depth):
        where = at_z(k + 1)
        span = pl.ds(pl.multiple_of(where * block, block), block)
        back_moves[k].wait_recv()
        total = part[y, span] + core_in[y, span].astype(jnp.float32) + y_in[k].astype(jnp.float32)
        if k < depth - 1:
            z_out[k] = total.astype(jnp.bfloat16)
            out_moves.append(send(z_out.at[k], z_in.at[k], rz_send.at[k], rz_recv.at[k], {"ctx": where}))
    def landed(where, k, slot):
        for far in (False, True):
            hands(here, where, slot, far)[-1].wait_recv()

    each_block(landed)

    @pl.loop(0, tokens // block)
    def _(c):
        span = pl.ds(pl.multiple_of(c * block, block), block)
        gate = gate_col[span, :]
        grads = rows[lax.div(c, depth), lax.rem(c, depth)].reshape(block, width)
        scaled_ref[span, :] = (gate * grads.astype(jnp.float32)).astype(jnp.bfloat16)

    for k in range(depth - 1):
        out_moves[k].wait_recv()
        total = total + z_in[k].astype(jnp.float32)
    for r in range(2):
        last[r] = total[r * tok:(r + 1) * tok].astype(jnp.bfloat16)
    finish = send(last.at[1 - d], halves.at[d], dp_send.at[3], dp_recv.at[3], other)
    halves[d] = last[d]
    finish.wait_recv()
    for half in range(2):
        combined_ref[:, half * width:(half + 1) * width] = halves[half]
    for copy in sent + [finish] + tz + ty + tc + core_moves + back_moves + out_moves:
        copy.wait_send()

    def left(where, k, slot):
        for ready, copy in onward(where, k, slot):
            pl.when(ready)(copy.wait_send)
        for copy in hands(here, where, slot, False) + hands(across, where, slot, True):
            copy.wait_send()

    each_block(left)


def fused_body(routed_experts, route_gates, expert_hidden, down_weight, output_grad):
    depth, lanes = lax.axis_size("ctx"), lax.axis_size("tp")
    tok, topk = routed_experts.shape
    capacity, ff = expert_hidden.shape[3:]
    sources = depth * lanes
    slots = sources * capacity
    width = output_grad.shape[1] // 2
    tokens = 2 * depth * lanes * tok
    per = tokens // lanes
    step = 512 if width % 512 == 0 else width
    vmem = pl.BlockSpec(memory_space=pltpu.VMEM)
    hbm = pl.BlockSpec(memory_space=pltpu.HBM)
    half = jnp.bfloat16
    dma = pltpu.SemaphoreType.DMA
    four, eight = dma((depth,)), dma((2 * depth,))
    combined, picked, scaled = pl.pallas_call(
        functools.partial(fused_kernel, (tok, topk, depth, lanes, ff, width, step)),
        out_shape=(
            jax.ShapeDtypeStruct(output_grad.shape, half),
            jax.ShapeDtypeStruct((2, 2 * per, ff), half),
            jax.ShapeDtypeStruct((tokens, width), half),
        ),
        in_specs=[vmem] * 2 + [hbm] * 3,
        out_specs=[vmem] * 3,
        scratch_shapes=[
            pltpu.VMEM((4 * topk, tok), jnp.float32),
            pltpu.VMEM((lanes, depth, 2, tok, 128), half),
            pltpu.VMEM((lanes, depth, 2, tok, width), half),
            pltpu.VMEM((2, slots, ff), half),
            pltpu.VMEM(down_weight.shape[1:], half),
            pltpu.VMEM((tokens, 1), jnp.float32),
            pltpu.VMEM((tokens, tokens), half),
            pltpu.VMEM((tokens, 1), jnp.float32),
            pltpu.VMEM((2, per, width), jnp.float32),
            pltpu.VMEM((2, per, width), half),
            pltpu.VMEM((2, per, width), half),
            pltpu.VMEM((depth, 2 * tok, width), half),
            pltpu.VMEM((depth, 2 * tok, width), half),
            pltpu.VMEM((depth, 2 * tok, width), half),
            pltpu.VMEM((depth, 2 * tok, width), half),
            pltpu.VMEM((2, tok, width), half),
            pltpu.VMEM((2, tok, width), half),
            dma((3,)), dma((4,)), dma((4,)), four, four, four, four, eight, eight,
            eight, eight, eight, eight, dma((4 * depth,)), dma((4 * depth,)),
            dma((2,)), dma((2,)), four, four, four, four,
        ],
        compiler_params=pltpu.CompilerParams(
            collective_id=0, has_side_effects=True, vmem_limit_bytes=58 * 1024 * 1024),
    )(
        routed_experts.T, route_gates.T, output_grad,
        expert_hidden[0, 0].transpose(1, 0, 2).reshape(slots, ff), down_weight[0])
    gradient = lax.dot_general(
        picked.reshape(tokens, ff), scaled, (((0,), (0,)), ((), ())), preferred_element_type=jnp.float32)
    return combined, gradient[None]


def solution(mesh):
    in_specs = (
        P(("dp", "ctx", "tp"), None),
        P(("dp", "ctx", "tp"), None),
        P(("ctx", "tp"), "dp", None, None, None),
        P(("ctx", "tp"), None, "dp"),
        P(("dp", "ctx", "tp"), None),
    )
    out_specs = (P(("dp", "ctx", "tp"), None), P(("ctx", "tp"), None, "dp"))
    pairs = mesh.shape["dp"] == 2 and mesh.shape["tp"] == 4
    return jax.shard_map(fused_body if pairs else body, mesh=mesh, in_specs=in_specs, out_specs=out_specs, check_vma=False)
```

```python
import functools

import jax
import jax.numpy as jnp
from jax import lax
from jax.experimental import pallas as pl
from jax.experimental.pallas import tpu as pltpu
from jax.sharding import PartitionSpec as P


def slot_ranks(flat_experts):
    count = flat_experts.shape[-1]
    same = flat_experts[..., :, None] == flat_experts[..., None, :]
    before = lax.broadcasted_iota(jnp.int32, (count, count), 1) < lax.broadcasted_iota(
        jnp.int32, (count, count), 0
    )
    return jnp.sum(jnp.logical_and(same, before), axis=-1)


def expert_move(buffer):
    return lax.all_to_all(buffer, ("ctx", "tp"), split_axis=0, concat_axis=0, tiled=True)


def body(routed_experts, route_gates, expert_hidden, down_weight, output_grad):
    replicas = lax.axis_size("dp")
    sources = lax.axis_size("ctx") * lax.axis_size("tp")
    tok_own, topk = routed_experts.shape
    routes = tok_own * topk
    capacity = expert_hidden.shape[3]
    width = output_grad.shape[1]
    column_part = width // replicas
    hidden_rows = expert_hidden[0]
    weight = down_weight[0]
    slot_count = sources * capacity
    expert_table, gate_table = (
        lax.all_gather(routed_experts.astype(jnp.float32), "dp", axis=0, tiled=True),
        lax.all_gather(route_gates, "dp", axis=0, tiled=True),
    )
    all_experts = expert_table.astype(jnp.int32).reshape(replicas, routes)
    all_gates = gate_table.reshape(replicas, tok_own, topk)
    grad_columns = lax.all_to_all(
        output_grad, "dp", split_axis=1, concat_axis=0, tiled=True
    ).reshape(replicas, tok_own, 1, column_part)
    ranks = slot_ranks(all_experts)
    target = all_experts * capacity + ranks
    placer = (
        lax.broadcasted_iota(jnp.int32, (1, slot_count, routes), 1) == target[:, None, :]
    ).astype(jnp.bfloat16)
    scaled = (
        (all_gates[:, :, :, None] * grad_columns.astype(jnp.float32))
        .reshape(replicas, routes, column_part)
        .astype(jnp.bfloat16)
    )
    outgoing = jnp.einsum("rpq,rqd->prd", placer, scaled, preferred_element_type=jnp.float32)
    outgoing = outgoing.astype(jnp.bfloat16).reshape(sources, capacity, replicas, column_part)
    grad_rows = expert_move(outgoing)
    piece = lax.all_gather(hidden_rows, "dp", axis=0, tiled=True)
    produced = jnp.einsum(
        "rsjf,fd->srjd", piece, weight, preferred_element_type=jnp.float32
    ).astype(jnp.bfloat16)
    outputs = produced
    gradient = jnp.einsum("rsjf,sjrd->fd", piece, grad_rows, preferred_element_type=jnp.float32)
    outputs, gradient = (outputs, gradient)
    returned = expert_move(outputs).reshape(sources * replicas * capacity, column_part)
    replica_index = lax.broadcasted_iota(jnp.int32, (replicas, routes), 0)
    position = all_experts * (replicas * capacity) + replica_index * capacity + ranks
    picked = (
        jnp.take(returned, position, axis=0)
        .astype(jnp.float32)
        .reshape(replicas, tok_own, topk, column_part)
    )
    partial_rows = jnp.sum(all_gates[:, :, :, None] * picked, axis=2).astype(jnp.bfloat16)
    combined = lax.all_to_all(partial_rows, "dp", split_axis=0, concat_axis=2, tiled=True)[0]
    return (combined, gradient[None])


MESH = pl.DeviceIdType.MESH


def fused_kernel(
    sizes, routes_ref, gates_ref, grad_ref, hidden_ref, weight_ref,
    combined_ref, tokens_out, scaled_out,
    tokens_ref, scaled_ref,
    stack, tables, rows, hidden, weight, base, lower, gate_col,
    part, core_out, core_in, y_out, y_in, z_out, z_in, last, halves,
    local_sem, dp_send, dp_recv, tz_send, tz_recv, ty_send, ty_recv, tc_send, tc_recv,
    z_send, z_recv, y_send, y_recv, c_send, c_recv,
    rc_send, rc_recv, ry_send, ry_recv, rz_send, rz_recv,
):
    tok, topk, depth, lanes, ff, width, step = sizes
    d, z, t = lax.axis_index("dp"), lax.axis_index("ctx"), lax.axis_index("tp")
    core = lax.rem(t, 2)
    y = lax.div(t, 2)
    other = {"dp": 1 - d}
    y_peer = {"tp": (1 - y) * 2 + core}
    c_peer = {"tp": y * 2 + 1 - core}
    here, across = core * 2 + y, core * 2 + 1 - y
    per = depth * 2 * tok
    block = 2 * tok
    tokens = lanes * per

    def at_z(k):
        return lax.rem(z + k, depth)

    def back(k):
        return lax.rem(z - k + depth, depth)

    def send(src, dst, send_sem, recv_sem, to):
        copy = pltpu.make_async_remote_copy(
            src_ref=src, dst_ref=dst, send_sem=send_sem, recv_sem=recv_sem,
            device_id=to, device_id_type=MESH)
        copy.start()
        return copy

    def columns_of(half):
        return grad_ref.at[:, pl.ds(pl.multiple_of(half * width, 128), width)]

    barrier = pltpu.get_barrier_semaphore()
    peers = [other, y_peer, c_peer] + [{"ctx": at_z(k)} for k in range(1, depth)]
    for peer in peers:
        pl.semaphore_signal(barrier, inc=1, device_id=peer, device_id_type=MESH)
    local = []
    for i, (src, dst) in enumerate((
        (columns_of(d), rows.at[here, z, d]), (hidden_ref, hidden.at[d]),
        (weight_ref, weight),
    )):
        local.append(pltpu.make_async_copy(src, dst, local_sem.at[i]))
        local[-1].start()
    gates = gates_ref[...]
    high = gates.astype(jnp.bfloat16).astype(jnp.float32)
    middle = (gates - high).astype(jnp.bfloat16).astype(jnp.float32)
    stack[0:topk] = routes_ref[...].astype(jnp.float32)
    stack[topk:2 * topk] = high
    stack[2 * topk:3 * topk] = middle
    stack[3 * topk:] = gates - high - middle
    spread_rows = lax.broadcasted_iota(jnp.int32, (4 * topk, 128), 0)
    spread_lanes = lax.broadcasted_iota(jnp.int32, (4 * topk, 128), 1)
    spreader = jnp.where(spread_rows == spread_lanes, 1.0, 0.0).astype(jnp.bfloat16)
    tables[here, z, d] = lax.dot_general(
        stack[...].astype(jnp.bfloat16), spreader, (((0,), (0,)), ((), ())),
        preferred_element_type=jnp.float32).astype(jnp.bfloat16)
    pl.semaphore_wait(barrier, len(peers))

    own = tables.at[here, z, d]
    sent = [send(own, own, dp_send.at[0], dp_recv.at[0], other)]
    sent.append(send(columns_of(1 - d), rows.at[here, z, d], dp_send.at[1], dp_recv.at[1], other))
    sent.append(send(hidden_ref, hidden.at[d], dp_send.at[2], dp_recv.at[2], other))

    def spread_z(buffer, sends, recvs):
        own = buffer.at[here, z]
        return [send(own, own, sends.at[k], recvs.at[k], {"ctx": at_z(k)}) for k in range(1, depth)]

    def hand(buffer, group, k, slot, sends, recvs, to):
        own = buffer.at[group, back(k)]
        return send(own, own, sends.at[slot], recvs.at[slot], to)

    sources = depth * lanes
    for q in range(lanes):
        for k in range(2 * depth):
            origin = k % 2 * (sources * (hidden.shape[1] // sources)) + k // 2 * lanes + q % 2 * 2 + q // 2
            start = q * per + k * tok
            base[start:start + tok] = jnp.full((tok, 1), float(origin), jnp.float32)
    lower_rows = lax.broadcasted_iota(jnp.int32, (tok, tokens), 0)
    lower_lanes = lax.broadcasted_iota(jnp.int32, (tok, tokens), 1)

    @pl.loop(0, tokens // tok)
    def _(c):
        earlier = jnp.logical_and(lower_lanes >= c * tok, lower_lanes < lower_rows + c * tok)
        lower[pl.ds(pl.multiple_of(c * tok, tok), tok), :] = jnp.where(earlier, 1.0, 0.0).astype(jnp.bfloat16)

    def line(where, k, leftward, to):
        own = rows.at[here, where]
        slot = depth + k if leftward else k
        return pltpu.make_async_remote_copy(
            src_ref=own, dst_ref=own, send_sem=z_send.at[slot], recv_sem=z_recv.at[slot],
            device_id={"ctx": to}, device_id_type=MESH)

    def hands(group, where, slot, far):
        own = rows.at[group, where]
        mine = 2 * depth + slot if far else slot
        to_core = pltpu.make_async_remote_copy(
            src_ref=own, dst_ref=own, send_sem=c_send.at[mine], recv_sem=c_recv.at[mine],
            device_id=c_peer, device_id_type=MESH)
        if far:
            return [to_core]
        return [pltpu.make_async_remote_copy(
            src_ref=own, dst_ref=own, send_sem=y_send.at[slot], recv_sem=y_recv.at[slot],
            device_id=y_peer, device_id_type=MESH), to_core]

    def onward(where, k, slot):
        moves = []
        if slot < depth:
            moves.append((z < depth - 1, line(where, k + 1, False, at_z(1))))
        if slot >= depth or k == 0:
            moves.append((z > 0, line(where, k + 1, True, back(1))))
        return moves if k + 1 < depth else []

    def pass_on(where, k, *slots):
        for ready, copy in onward(where, k, 0) if k == 0 else onward(where, k, slots[0]):
            pl.when(ready)(copy.start)
        for copy in hands(here, where, 0 if k == 0 else slots[0], False):
            copy.start()

    def arrivals(k):
        return ((z >= k, back(k), k), (z + k < depth, at_z(k), depth + k))

    def relay(k):
        for valid, where, slot in arrivals(k):
            @pl.when(valid)
            def _(where=where, slot=slot):
                line(where, k, slot >= depth, at_z(1)).wait_recv()
                pass_on(where, k, slot)

    def each_block(act):
        act(z, 0, 0)
        for k in range(1, depth):
            for valid, where, slot in arrivals(k):
                @pl.when(valid)
                def _(where=where, slot=slot, k=k):
                    act(where, k, slot)

    sent[0].wait_recv()
    tz = spread_z(tables, tz_send, tz_recv)
    ty, tc = [], []
    ty.append(hand(tables, here, 0, 0, ty_send, ty_recv, y_peer))
    tc.append(hand(tables, here, 0, 0, tc_send, tc_recv, c_peer))
    local[0].wait()
    sent[1].wait_recv()
    pass_on(z, 0)
    for k in range(1, depth):
        tz[k - 1].wait_recv()
        ty.append(hand(tables, here, k, k, ty_send, ty_recv, y_peer))
        tc.append(hand(tables, here, k, k, tc_send, tc_recv, c_peer))
    for k in range(depth):
        ty[k].wait_recv()
        tc.append(hand(tables, across, k, depth + k, tc_send, tc_recv, c_peer))
    relay(1)
    for copy in tc:
        copy.wait_recv()

    expert = (z * lanes + t).astype(jnp.float32)
    table = tables[...].reshape(tokens, 128).astype(jnp.float32)
    lane = lax.broadcasted_iota(jnp.int32, (tokens, 128), 1)
    named = jnp.where(jnp.logical_and(lane < topk, table == expert), 1.0, 0.0)
    spread = pltpu.roll(named, topk, 1) + pltpu.roll(named, 2 * topk, 1) + pltpu.roll(named, 3 * topk, 1)
    gate_col[...] = jnp.sum(spread * table, axis=1, keepdims=True)
    before = jnp.dot(lower[...], named.astype(jnp.bfloat16), preferred_element_type=jnp.float32)
    rank = jnp.sum(before, axis=1, keepdims=True)
    used = jnp.sum(named, axis=1, keepdims=True) > 0.5
    slot = jnp.where(used, base[...] + rank * (depth * lanes), -1.0)
    slots = 2 * hidden.shape[1]
    place = lax.broadcasted_iota(jnp.int32, (tokens, slots), 1).astype(jnp.float32)
    placer = jnp.where(place == slot, 1.0, 0.0).astype(jnp.bfloat16)
    local[1].wait()
    sent[2].wait_recv()
    picked = jnp.dot(placer, hidden[...].reshape(slots, ff), preferred_element_type=jnp.float32)
    tokens_ref[...] = picked.astype(jnp.bfloat16).reshape(tokens_ref.shape)
    keep_tokens = pltpu.make_async_copy(tokens_ref, tokens_out, local_sem.at[3])
    keep_tokens.start()
    relay(2)
    local[2].wait()

    def forward(side, out):
        left = tokens_ref[side]
        gate = gate_col[pl.ds(pl.multiple_of(side * 2 * per, per), 2 * per), :]

        @pl.loop(0, width // step)
        def _(c):
            columns = pl.ds(pl.multiple_of(c * step, step), step)
            made = jnp.dot(left, weight[:, columns], preferred_element_type=jnp.float32)
            made = made.astype(jnp.bfloat16).astype(jnp.float32) * gate
            for half in range(2):
                out[half, :, columns] = made[half * per:(half + 1) * per].astype(out.dtype)

    forward(1 - core, core_out)
    core_moves = []
    for i, side in enumerate((1 - y, y)):
        core_moves.append(send(core_out.at[side], core_in.at[side], rc_send.at[i], rc_recv.at[i], c_peer))
    forward(core, part)
    for k in range(3, depth):
        relay(k)
    core_moves[0].wait_recv()
    back_moves = []
    for k in range(depth):
        span = pl.ds(pl.multiple_of(at_z(k + 1) * block, block), block)
        y_out[k] = (part[1 - y, span] + core_in[1 - y, span].astype(jnp.float32)).astype(jnp.bfloat16)
        back_moves.append(send(y_out.at[k], y_in.at[k], ry_send.at[k], ry_recv.at[k], y_peer))
    def cross(where, k, slot):
        hands(here, where, slot, False)[0].wait_recv()
        hands(across, where, slot, True)[0].start()

    each_block(cross)
    core_moves[1].wait_recv()
    out_moves = []
    for k in range(depth):
        where = at_z(k + 1)
        span = pl.ds(pl.multiple_of(where * block, block), block)
        back_moves[k].wait_recv()
        total = part[y, span] + core_in[y, span].astype(jnp.float32) + y_in[k].astype(jnp.float32)
        if k < depth - 1:
            z_out[k] = total.astype(jnp.bfloat16)
            out_moves.append(send(z_out.at[k], z_in.at[k], rz_send.at[k], rz_recv.at[k], {"ctx": where}))
    def landed(where, k, slot):
        for far in (False, True):
            hands(here, where, slot, far)[-1].wait_recv()

    each_block(landed)

    @pl.loop(0, tokens // block)
    def _(c):
        span = pl.ds(pl.multiple_of(c * block, block), block)
        gate = gate_col[span, :]
        grads = rows[lax.div(c, depth), lax.rem(c, depth)].reshape(block, width)
        scaled_ref[span, :] = (gate * grads.astype(jnp.float32)).astype(jnp.bfloat16)

    keep_scaled = pltpu.make_async_copy(scaled_ref, scaled_out, local_sem.at[4])
    keep_scaled.start()
    for k in range(depth - 1):
        out_moves[k].wait_recv()
        total = total + z_in[k].astype(jnp.float32)
    for r in range(2):
        last[r] = total[r * tok:(r + 1) * tok].astype(jnp.bfloat16)
    finish = send(last.at[1 - d], halves.at[d], dp_send.at[3], dp_recv.at[3], other)
    halves[d] = last[d]
    finish.wait_recv()
    for half in range(2):
        combined_ref[:, half * width:(half + 1) * width] = halves[half]
    for copy in sent + [finish] + tz + ty + tc + core_moves + back_moves + out_moves:
        copy.wait_send()

    def left(where, k, slot):
        for ready, copy in onward(where, k, slot):
            pl.when(ready)(copy.wait_send)
        for copy in hands(here, where, slot, False) + hands(across, where, slot, True):
            copy.wait_send()

    each_block(left)
    keep_tokens.wait()
    keep_scaled.wait()


def fused_body(routed_experts, route_gates, expert_hidden, down_weight, output_grad):
    depth, lanes = lax.axis_size("ctx"), lax.axis_size("tp")
    tok, topk = routed_experts.shape
    capacity, ff = expert_hidden.shape[3:]
    sources = depth * lanes
    slots = sources * capacity
    width = output_grad.shape[1] // 2
    tokens = 2 * depth * lanes * tok
    per = tokens // lanes
    step = 512 if width % 512 == 0 else width
    vmem = pl.BlockSpec(memory_space=pltpu.VMEM)
    hbm = pl.BlockSpec(memory_space=pltpu.HBM)
    half = jnp.bfloat16
    dma = pltpu.SemaphoreType.DMA
    four, eight = dma((depth,)), dma((2 * depth,))
    combined, picked, scaled = pl.pallas_call(
        functools.partial(fused_kernel, (tok, topk, depth, lanes, ff, width, step)),
        out_shape=(
            jax.ShapeDtypeStruct(output_grad.shape, half),
            jax.ShapeDtypeStruct((2, 2 * per, ff), half),
            jax.ShapeDtypeStruct((tokens, width), half),
        ),
        in_specs=[vmem] * 2 + [hbm] * 3,
        out_specs=[vmem, hbm, hbm],
        scratch_shapes=[
            pltpu.VMEM((2, 2 * per, ff), half),
            pltpu.VMEM((tokens, width), half),
            pltpu.VMEM((4 * topk, tok), jnp.float32),
            pltpu.VMEM((lanes, depth, 2, tok, 128), half),
            pltpu.VMEM((lanes, depth, 2, tok, width), half),
            pltpu.VMEM((2, slots, ff), half),
            pltpu.VMEM(down_weight.shape[1:], half),
            pltpu.VMEM((tokens, 1), jnp.float32),
            pltpu.VMEM((tokens, tokens), half),
            pltpu.VMEM((tokens, 1), jnp.float32),
            pltpu.VMEM((2, per, width), jnp.float32),
            pltpu.VMEM((2, per, width), half),
            pltpu.VMEM((2, per, width), half),
            pltpu.VMEM((depth, 2 * tok, width), half),
            pltpu.VMEM((depth, 2 * tok, width), half),
            pltpu.VMEM((depth, 2 * tok, width), half),
            pltpu.VMEM((depth, 2 * tok, width), half),
            pltpu.VMEM((2, tok, width), half),
            pltpu.VMEM((2, tok, width), half),
            dma((5,)), dma((4,)), dma((4,)), four, four, four, four, eight, eight,
            eight, eight, eight, eight, dma((4 * depth,)), dma((4 * depth,)),
            dma((2,)), dma((2,)), four, four, four, four,
        ],
        compiler_params=pltpu.CompilerParams(
            collective_id=0, has_side_effects=True, vmem_limit_bytes=58 * 1024 * 1024),
    )(
        routed_experts.T, route_gates.T, output_grad,
        expert_hidden[0, 0].transpose(1, 0, 2).reshape(slots, ff), down_weight[0])
    gradient = lax.dot_general(
        picked.reshape(tokens, ff), scaled, (((0,), (0,)), ((), ())), preferred_element_type=jnp.float32)
    return combined, gradient[None]


def solution(mesh):
    in_specs = (
        P(("dp", "ctx", "tp"), None),
        P(("dp", "ctx", "tp"), None),
        P(("ctx", "tp"), "dp", None, None, None),
        P(("ctx", "tp"), None, "dp"),
        P(("dp", "ctx", "tp"), None),
    )
    out_specs = (P(("dp", "ctx", "tp"), None), P(("ctx", "tp"), None, "dp"))
    pairs = mesh.shape["dp"] == 2 and mesh.shape["tp"] == 4
    return jax.shard_map(fused_body if pairs else body, mesh=mesh, in_specs=in_specs, out_specs=out_specs, check_vma=False)
```

```python
import functools

import jax
import jax.numpy as jnp
from jax import lax
from jax.experimental import pallas as pl
from jax.experimental.pallas import tpu as pltpu
from jax.sharding import PartitionSpec as P


def slot_ranks(flat_experts):
    count = flat_experts.shape[-1]
    same = flat_experts[..., :, None] == flat_experts[..., None, :]
    before = lax.broadcasted_iota(jnp.int32, (count, count), 1) < lax.broadcasted_iota(
        jnp.int32, (count, count), 0
    )
    return jnp.sum(jnp.logical_and(same, before), axis=-1)


def expert_move(buffer):
    return lax.all_to_all(buffer, ("ctx", "tp"), split_axis=0, concat_axis=0, tiled=True)


def body(routed_experts, route_gates, expert_hidden, down_weight, output_grad):
    replicas = lax.axis_size("dp")
    sources = lax.axis_size("ctx") * lax.axis_size("tp")
    tok_own, topk = routed_experts.shape
    routes = tok_own * topk
    capacity = expert_hidden.shape[3]
    width = output_grad.shape[1]
    column_part = width // replicas
    hidden_rows = expert_hidden[0]
    weight = down_weight[0]
    slot_count = sources * capacity
    expert_table, gate_table = (
        lax.all_gather(routed_experts.astype(jnp.float32), "dp", axis=0, tiled=True),
        lax.all_gather(route_gates, "dp", axis=0, tiled=True),
    )
    all_experts = expert_table.astype(jnp.int32).reshape(replicas, routes)
    all_gates = gate_table.reshape(replicas, tok_own, topk)
    grad_columns = lax.all_to_all(
        output_grad, "dp", split_axis=1, concat_axis=0, tiled=True
    ).reshape(replicas, tok_own, 1, column_part)
    ranks = slot_ranks(all_experts)
    target = all_experts * capacity + ranks
    placer = (
        lax.broadcasted_iota(jnp.int32, (1, slot_count, routes), 1) == target[:, None, :]
    ).astype(jnp.bfloat16)
    scaled = (
        (all_gates[:, :, :, None] * grad_columns.astype(jnp.float32))
        .reshape(replicas, routes, column_part)
        .astype(jnp.bfloat16)
    )
    outgoing = jnp.einsum("rpq,rqd->prd", placer, scaled, preferred_element_type=jnp.float32)
    outgoing = outgoing.astype(jnp.bfloat16).reshape(sources, capacity, replicas, column_part)
    grad_rows = expert_move(outgoing)
    piece = lax.all_gather(hidden_rows, "dp", axis=0, tiled=True)
    produced = jnp.einsum(
        "rsjf,fd->srjd", piece, weight, preferred_element_type=jnp.float32
    ).astype(jnp.bfloat16)
    outputs = produced
    gradient = jnp.einsum("rsjf,sjrd->fd", piece, grad_rows, preferred_element_type=jnp.float32)
    outputs, gradient = (outputs, gradient)
    returned = expert_move(outputs).reshape(sources * replicas * capacity, column_part)
    replica_index = lax.broadcasted_iota(jnp.int32, (replicas, routes), 0)
    position = all_experts * (replicas * capacity) + replica_index * capacity + ranks
    picked = (
        jnp.take(returned, position, axis=0)
        .astype(jnp.float32)
        .reshape(replicas, tok_own, topk, column_part)
    )
    partial_rows = jnp.sum(all_gates[:, :, :, None] * picked, axis=2).astype(jnp.bfloat16)
    combined = lax.all_to_all(partial_rows, "dp", split_axis=0, concat_axis=2, tiled=True)[0]
    return (combined, gradient[None])


MESH = pl.DeviceIdType.MESH


def fused_kernel(
    sizes, routes_ref, gates_ref, grad_ref, hidden_ref, weight_ref,
    combined_ref, tokens_out, scaled_out,
    tokens_ref, scaled_ref,
    stack, tables, rows, hidden, weight, base, lower, gate_col,
    part, core_out, core_in, y_out, y_in, z_out, z_in, last, halves,
    local_sem, dp_send, dp_recv, tz_send, tz_recv, ty_send, ty_recv, tc_send, tc_recv,
    z_send, z_recv, y_send, y_recv, c_send, c_recv,
    rc_send, rc_recv, ry_send, ry_recv, rz_send, rz_recv,
):
    tok, topk, depth, lanes, ff, width, step = sizes
    d, z, t = lax.axis_index("dp"), lax.axis_index("ctx"), lax.axis_index("tp")
    core = lax.rem(t, 2)
    y = lax.div(t, 2)
    other = {"dp": 1 - d}
    y_peer = {"tp": (1 - y) * 2 + core}
    c_peer = {"tp": y * 2 + 1 - core}
    here, across = core * 2 + y, core * 2 + 1 - y
    per = depth * 2 * tok
    block = 2 * tok
    tokens = lanes * per

    def at_z(k):
        return lax.rem(z + k, depth)

    def back(k):
        return lax.rem(z - k + depth, depth)

    def send(src, dst, send_sem, recv_sem, to):
        copy = pltpu.make_async_remote_copy(
            src_ref=src, dst_ref=dst, send_sem=send_sem, recv_sem=recv_sem,
            device_id=to, device_id_type=MESH)
        copy.start()
        return copy

    def columns_of(half):
        return grad_ref.at[:, pl.ds(pl.multiple_of(half * width, 128), width)]

    barrier = pltpu.get_barrier_semaphore()
    peers = [other, y_peer, c_peer] + [{"ctx": at_z(k)} for k in range(1, depth)]
    for peer in peers:
        pl.semaphore_signal(barrier, inc=1, device_id=peer, device_id_type=MESH)
    local = []
    for i, (src, dst) in enumerate((
        (columns_of(d), rows.at[here, z, d]), (hidden_ref, hidden.at[d]),
        (weight_ref, weight),
    )):
        local.append(pltpu.make_async_copy(src, dst, local_sem.at[i]))
        local[-1].start()
    gates = gates_ref[...]
    high = gates.astype(jnp.bfloat16).astype(jnp.float32)
    middle = (gates - high).astype(jnp.bfloat16).astype(jnp.float32)
    stack[0:topk] = routes_ref[...].astype(jnp.float32)
    stack[topk:2 * topk] = high
    stack[2 * topk:3 * topk] = middle
    stack[3 * topk:] = gates - high - middle
    spread_rows = lax.broadcasted_iota(jnp.int32, (4 * topk, 128), 0)
    spread_lanes = lax.broadcasted_iota(jnp.int32, (4 * topk, 128), 1)
    spreader = jnp.where(spread_rows == spread_lanes, 1.0, 0.0).astype(jnp.bfloat16)
    tables[here, z, d] = lax.dot_general(
        stack[...].astype(jnp.bfloat16), spreader, (((0,), (0,)), ((), ())),
        preferred_element_type=jnp.float32).astype(jnp.bfloat16)
    pl.semaphore_wait(barrier, len(peers))

    own = tables.at[here, z, d]
    sent = [send(own, own, dp_send.at[0], dp_recv.at[0], other)]
    sent.append(send(columns_of(1 - d), rows.at[here, z, d], dp_send.at[1], dp_recv.at[1], other))
    sent.append(send(hidden_ref, hidden.at[d], dp_send.at[2], dp_recv.at[2], other))

    def spread_z(buffer, sends, recvs):
        own = buffer.at[here, z]
        return [send(own, own, sends.at[k], recvs.at[k], {"ctx": at_z(k)}) for k in range(1, depth)]

    def hand(buffer, group, k, slot, sends, recvs, to):
        own = buffer.at[group, back(k)]
        return send(own, own, sends.at[slot], recvs.at[slot], to)

    sources = depth * lanes
    for q in range(lanes):
        for k in range(2 * depth):
            origin = k % 2 * (sources * (hidden.shape[1] // sources)) + k // 2 * lanes + q % 2 * 2 + q // 2
            start = q * per + k * tok
            base[start:start + tok] = jnp.full((tok, 1), float(origin), jnp.float32)
    lower_rows = lax.broadcasted_iota(jnp.int32, (tok, tokens), 0)
    lower_lanes = lax.broadcasted_iota(jnp.int32, (tok, tokens), 1)

    @pl.loop(0, tokens // tok)
    def _(c):
        earlier = jnp.logical_and(lower_lanes >= c * tok, lower_lanes < lower_rows + c * tok)
        lower[pl.ds(pl.multiple_of(c * tok, tok), tok), :] = jnp.where(earlier, 1.0, 0.0).astype(jnp.bfloat16)

    def line(where, k, leftward, to):
        own = rows.at[here, where]
        slot = depth + k if leftward else k
        return pltpu.make_async_remote_copy(
            src_ref=own, dst_ref=own, send_sem=z_send.at[slot], recv_sem=z_recv.at[slot],
            device_id={"ctx": to}, device_id_type=MESH)

    def hands(group, where, slot, far):
        own = rows.at[group, where]
        mine = 2 * depth + slot if far else slot
        to_core = pltpu.make_async_remote_copy(
            src_ref=own, dst_ref=own, send_sem=c_send.at[mine], recv_sem=c_recv.at[mine],
            device_id=c_peer, device_id_type=MESH)
        if far:
            return [to_core]
        return [pltpu.make_async_remote_copy(
            src_ref=own, dst_ref=own, send_sem=y_send.at[slot], recv_sem=y_recv.at[slot],
            device_id=y_peer, device_id_type=MESH), to_core]

    def onward(where, k, slot):
        moves = []
        if slot < depth:
            moves.append((z < depth - 1, line(where, k + 1, False, at_z(1))))
        if slot >= depth or k == 0:
            moves.append((z > 0, line(where, k + 1, True, back(1))))
        return moves if k + 1 < depth else []

    def pass_on(where, k, *slots):
        for ready, copy in onward(where, k, 0) if k == 0 else onward(where, k, slots[0]):
            pl.when(ready)(copy.start)
        for copy in hands(here, where, 0 if k == 0 else slots[0], False):
            copy.start()

    def arrivals(k):
        return ((z >= k, back(k), k), (z + k < depth, at_z(k), depth + k))

    def relay(k):
        for valid, where, slot in arrivals(k):
            @pl.when(valid)
            def _(where=where, slot=slot):
                line(where, k, slot >= depth, at_z(1)).wait_recv()
                pass_on(where, k, slot)

    def each_block(act):
        act(z, 0, 0)
        for k in range(1, depth):
            for valid, where, slot in arrivals(k):
                @pl.when(valid)
                def _(where=where, slot=slot, k=k):
                    act(where, k, slot)

    sent[0].wait_recv()
    tz = spread_z(tables, tz_send, tz_recv)
    ty, tc = [], []
    ty.append(hand(tables, here, 0, 0, ty_send, ty_recv, y_peer))
    tc.append(hand(tables, here, 0, 0, tc_send, tc_recv, c_peer))
    local[0].wait()
    sent[1].wait_recv()
    pass_on(z, 0)
    for k in range(1, depth):
        tz[k - 1].wait_recv()
        ty.append(hand(tables, here, k, k, ty_send, ty_recv, y_peer))
        tc.append(hand(tables, here, k, k, tc_send, tc_recv, c_peer))
    for k in range(depth):
        ty[k].wait_recv()
        tc.append(hand(tables, across, k, depth + k, tc_send, tc_recv, c_peer))
    relay(1)
    for copy in tc:
        copy.wait_recv()

    expert = (z * lanes + t).astype(jnp.float32)
    table = tables[...].reshape(tokens, 128).astype(jnp.float32)
    lane = lax.broadcasted_iota(jnp.int32, (tokens, 128), 1)
    named = jnp.where(jnp.logical_and(lane < topk, table == expert), 1.0, 0.0)
    spread = pltpu.roll(named, topk, 1) + pltpu.roll(named, 2 * topk, 1) + pltpu.roll(named, 3 * topk, 1)
    gate_col[...] = jnp.sum(spread * table, axis=1, keepdims=True)
    before = jnp.dot(lower[...], named.astype(jnp.bfloat16), preferred_element_type=jnp.float32)
    rank = jnp.sum(before, axis=1, keepdims=True)
    used = jnp.sum(named, axis=1, keepdims=True) > 0.5
    slot = jnp.where(used, base[...] + rank * (depth * lanes), -1.0)
    slots = 2 * hidden.shape[1]
    place = lax.broadcasted_iota(jnp.int32, (tokens, slots), 1).astype(jnp.float32)
    placer = jnp.where(place == slot, 1.0, 0.0).astype(jnp.bfloat16)
    local[1].wait()
    sent[2].wait_recv()
    picked = jnp.dot(placer, hidden[...].reshape(slots, ff), preferred_element_type=jnp.float32)
    tokens_ref[...] = picked.astype(jnp.bfloat16).reshape(tokens_ref.shape)
    keep_tokens = pltpu.make_async_copy(tokens_ref, tokens_out, local_sem.at[3])
    keep_tokens.start()
    relay(2)
    local[2].wait()

    def forward(side, out):
        left = tokens_ref[side]
        gate = gate_col[pl.ds(pl.multiple_of(side * 2 * per, per), 2 * per), :]

        @pl.loop(0, width // step)
        def _(c):
            columns = pl.ds(pl.multiple_of(c * step, step), step)
            made = jnp.dot(left, weight[:, columns], preferred_element_type=jnp.float32)
            made = made.astype(jnp.bfloat16).astype(jnp.float32) * gate
            for half in range(2):
                out[half, :, columns] = made[half * per:(half + 1) * per].astype(out.dtype)

    forward(1 - core, core_out)
    core_moves = []
    for i, side in enumerate((1 - y, y)):
        core_moves.append(send(core_out.at[side], core_in.at[side], rc_send.at[i], rc_recv.at[i], c_peer))
    forward(core, part)
    core_moves[0].wait_recv()
    back_moves = []
    for k in range(depth):
        span = pl.ds(pl.multiple_of(at_z(k + 1) * block, block), block)
        y_out[k] = (part[1 - y, span] + core_in[1 - y, span].astype(jnp.float32)).astype(jnp.bfloat16)
        back_moves.append(send(y_out.at[k], y_in.at[k], ry_send.at[k], ry_recv.at[k], y_peer))
    for k in range(3, depth):
        relay(k)

    def cross(where, k, slot):
        hands(here, where, slot, False)[0].wait_recv()
        hands(across, where, slot, True)[0].start()

    each_block(cross)
    core_moves[1].wait_recv()
    out_moves = []
    for k in range(depth):
        where = at_z(k + 1)
        span = pl.ds(pl.multiple_of(where * block, block), block)
        back_moves[k].wait_recv()
        total = part[y, span] + core_in[y, span].astype(jnp.float32) + y_in[k].astype(jnp.float32)
        if k < depth - 1:
            z_out[k] = total.astype(jnp.bfloat16)
            out_moves.append(send(z_out.at[k], z_in.at[k], rz_send.at[k], rz_recv.at[k], {"ctx": where}))
    def landed(where, k, slot):
        for far in (False, True):
            hands(here, where, slot, far)[-1].wait_recv()

    each_block(landed)

    @pl.loop(0, tokens // block)
    def _(c):
        span = pl.ds(pl.multiple_of(c * block, block), block)
        gate = gate_col[span, :]
        grads = rows[lax.div(c, depth), lax.rem(c, depth)].reshape(block, width)
        scaled_ref[span, :] = (gate * grads.astype(jnp.float32)).astype(jnp.bfloat16)

    keep_scaled = pltpu.make_async_copy(scaled_ref, scaled_out, local_sem.at[4])
    keep_scaled.start()
    for k in range(depth - 1):
        out_moves[k].wait_recv()
        total = total + z_in[k].astype(jnp.float32)
    for r in range(2):
        last[r] = total[r * tok:(r + 1) * tok].astype(jnp.bfloat16)
    finish = send(last.at[1 - d], halves.at[d], dp_send.at[3], dp_recv.at[3], other)
    halves[d] = last[d]
    finish.wait_recv()
    for half in range(2):
        combined_ref[:, half * width:(half + 1) * width] = halves[half]
    for copy in sent + [finish] + tz + ty + tc + core_moves + back_moves + out_moves:
        copy.wait_send()

    def left(where, k, slot):
        for ready, copy in onward(where, k, slot):
            pl.when(ready)(copy.wait_send)
        for copy in hands(here, where, slot, False) + hands(across, where, slot, True):
            copy.wait_send()

    each_block(left)
    keep_tokens.wait()
    keep_scaled.wait()


def fused_body(routed_experts, route_gates, expert_hidden, down_weight, output_grad):
    depth, lanes = lax.axis_size("ctx"), lax.axis_size("tp")
    tok, topk = routed_experts.shape
    capacity, ff = expert_hidden.shape[3:]
    sources = depth * lanes
    slots = sources * capacity
    width = output_grad.shape[1] // 2
    tokens = 2 * depth * lanes * tok
    per = tokens // lanes
    step = 512 if width % 512 == 0 else width
    vmem = pl.BlockSpec(memory_space=pltpu.VMEM)
    hbm = pl.BlockSpec(memory_space=pltpu.HBM)
    half = jnp.bfloat16
    dma = pltpu.SemaphoreType.DMA
    four, eight = dma((depth,)), dma((2 * depth,))
    combined, picked, scaled = pl.pallas_call(
        functools.partial(fused_kernel, (tok, topk, depth, lanes, ff, width, step)),
        out_shape=(
            jax.ShapeDtypeStruct(output_grad.shape, half),
            jax.ShapeDtypeStruct((2, 2 * per, ff), half),
            jax.ShapeDtypeStruct((tokens, width), half),
        ),
        in_specs=[vmem] * 2 + [hbm] * 3,
        out_specs=[vmem, hbm, hbm],
        scratch_shapes=[
            pltpu.VMEM((2, 2 * per, ff), half),
            pltpu.VMEM((tokens, width), half),
            pltpu.VMEM((4 * topk, tok), jnp.float32),
            pltpu.VMEM((lanes, depth, 2, tok, 128), half),
            pltpu.VMEM((lanes, depth, 2, tok, width), half),
            pltpu.VMEM((2, slots, ff), half),
            pltpu.VMEM(down_weight.shape[1:], half),
            pltpu.VMEM((tokens, 1), jnp.float32),
            pltpu.VMEM((tokens, tokens), half),
            pltpu.VMEM((tokens, 1), jnp.float32),
            pltpu.VMEM((2, per, width), jnp.float32),
            pltpu.VMEM((2, per, width), half),
            pltpu.VMEM((2, per, width), half),
            pltpu.VMEM((depth, 2 * tok, width), half),
            pltpu.VMEM((depth, 2 * tok, width), half),
            pltpu.VMEM((depth, 2 * tok, width), half),
            pltpu.VMEM((depth, 2 * tok, width), half),
            pltpu.VMEM((2, tok, width), half),
            pltpu.VMEM((2, tok, width), half),
            dma((5,)), dma((4,)), dma((4,)), four, four, four, four, eight, eight,
            eight, eight, eight, eight, dma((4 * depth,)), dma((4 * depth,)),
            dma((2,)), dma((2,)), four, four, four, four,
        ],
        compiler_params=pltpu.CompilerParams(
            collective_id=0, has_side_effects=True, vmem_limit_bytes=58 * 1024 * 1024),
    )(
        routed_experts.T, route_gates.T, output_grad,
        expert_hidden[0, 0].transpose(1, 0, 2).reshape(slots, ff), down_weight[0])
    gradient = lax.dot_general(
        picked.reshape(tokens, ff), scaled, (((0,), (0,)), ((), ())), preferred_element_type=jnp.float32)
    return combined, gradient[None]


def solution(mesh):
    in_specs = (
        P(("dp", "ctx", "tp"), None),
        P(("dp", "ctx", "tp"), None),
        P(("ctx", "tp"), "dp", None, None, None),
        P(("ctx", "tp"), None, "dp"),
        P(("dp", "ctx", "tp"), None),
    )
    out_specs = (P(("dp", "ctx", "tp"), None), P(("ctx", "tp"), None, "dp"))
    pairs = mesh.shape["dp"] == 2 and mesh.shape["tp"] == 4
    return jax.shard_map(fused_body if pairs else body, mesh=mesh, in_specs=in_specs, out_specs=out_specs, check_vma=False)
```
